32 devices in a mesh: dp: 16 (over z, x, core), tensor: 2 (over y).
Axes of the slice: x: 2, y: 2, z: 4, core: 2. Of those that a mesh axis runs over, the one named last changes fastest.
Arguments:
- gate_pre: bfloat16 [8192, 13312], P('dp', 'tensor'), may hold values from -6 to 6
- up_pre: bfloat16 [8192, 13312], P('dp', 'tensor'), may hold values from -6 to 6
- out_grad: bfloat16 [8192, 5120], P('dp', 'tensor'), may hold values from -0.06591797 to 0.06591797
- master: float32 [5120, 13312], P('dp', 'tensor'), may hold values from -6 to 6
- moment_one: float32 [5120, 13312], P('dp', 'tensor'), may hold values from -3 to 3
- moment_two: float32 [5120, 13312], P('dp', 'tensor'), may hold values from 0.05 to 1
Outputs:
- master_new: float32 [5120, 13312], P('dp', 'tensor')
- moment_one_new: float32 [5120, 13312], P('dp', 'tensor')
- moment_two_new: float32 [5120, 13312], P('dp', 'tensor')
- serving: bfloat16 [5120, 13312], P(('dp', 'tensor'))
The draws below stay inside these ranges and needn't reach their ends.
All inputs are finite; a program needn't handle non-finite values.
Results may differ from the reference program's by a relative error of at most 0.006.
Values may be sent and summed in bfloat16 or wider, within the bound.
A program may use at most 320 MiB of HBM per device.

```python
import math
import jax
import jax.numpy as jnp
from jax import lax

D = 5120
FF = 13312
TOK_DEV = 512
TOKENS = 8192
N_DP = 16


def spiked(array, rng, source, target, shards_of, factor):
    def block_of(position):
        return (jnp.arange(array.shape[position]) // (array.shape[position] // shards_of)).reshape((-1,) + (1,) * (array.ndim - 1 - position))

    one_side = jax.random.permutation(rng, shards_of)[block_of(target)]
    other_side = (block_of(target) + shards_of // 2) % shards_of
    return jnp.where((block_of(source) == one_side) | (block_of(source) == other_side), factor * array, array)


def block_levels(own_key, dims, pieces, low, high):
    def one(dim, parts):
        heights = jax.random.uniform(jax.random.fold_in(jax.random.fold_in(own_key, 6), dim), (parts,), jnp.float32, low / len(pieces), high / len(pieces))
        return jnp.repeat(jnp.exp(heights), dims[dim] // parts).reshape((-1,) + (1,) * (len(dims) - dim - 1))

    level = one(*pieces[0])
    for cut in pieces[1:]:
        level = level * one(*cut)
    return level


def noise(stream_key, extent, width, limit, shards=(), dtype=jnp.bfloat16):
    drawn = jax.random.normal(stream_key, extent, jnp.float32) * width
    if len(shards) > 0:
        drawn = block_levels(stream_key, extent, shards, -0.22, 0.18) * drawn
    return jnp.clip(drawn, min=-limit, max=limit).astype(dtype)


def noise_with(rng, extent, width, most, pieces, heavy, kind=jnp.bfloat16):
    values = width * jax.random.normal(rng, extent, jnp.float32)
    if pieces:
        values = values * block_levels(rng, extent, pieces, -0.22, 0.18)
    return jnp.clip(spiked(values, jax.random.fold_in(rng, 3), *heavy), -most, most).astype(kind)


def setup_inputs(seed: int = 0) -> dict:
    arg_keys = jax.random.split(jax.random.key(seed), 7)
    gate_pre = noise(arg_keys[0], (TOKENS, FF), 1.0, 6.0, ((0, 16), (1, 2)))
    up_pre = noise(arg_keys[1], (TOKENS, FF), 1.0, 6.0, ((0, 16), (1, 2)))
    out_grad = noise_with(arg_keys[2], (TOKENS, D), (TOKENS ** -0.5), 0.06591797, ((0, 16), (1, 2)), (0, 1, 16, 2.0))
    master = noise(arg_keys[3], (D, FF), 1.0, 6.0, ((0, 16), (1, 2)), jnp.float32)
    moment_one = noise(arg_keys[4], (D, FF), 0.5, 3.0, ((0, 16), (1, 2)), jnp.float32)
    moment_two = jnp.clip(jnp.exp(math.log(1.0) - 2.9957323 * jax.random.uniform(arg_keys[5], (D, FF), jnp.float32) ** block_levels(arg_keys[5], (D, FF), ((0, 16), (1, 2)), -0.2, 0.2)), 0.05, 1.0)
    return dict(gate_pre=gate_pre, up_pre=up_pre, out_grad=out_grad, master=master, moment_one=moment_one, moment_two=moment_two)


def reference(gate_pre, up_pre, out_grad, master, moment_one, moment_two):
    hidden = (jax.nn.silu(gate_pre.astype(jnp.float32)) * up_pre.astype(jnp.float32)).astype(jnp.bfloat16)
    hidden_blocks = hidden.reshape(N_DP, TOK_DEV, FF)
    grad_blocks = out_grad.reshape(N_DP, TOK_DEV, D)

    def accumulate(total, pair):
        left, right = pair
        partial_value = jnp.dot(left.astype(jnp.float32).T, right.astype(jnp.float32), precision=lax.Precision.HIGHEST, preferred_element_type=jnp.float32)
        rounded = lax.optimization_barrier(partial_value.astype(jnp.bfloat16))
        return (total + rounded.astype(jnp.float32), None)
    grad, _ = lax.scan(accumulate, jnp.zeros((D, FF), jnp.float32), (grad_blocks, hidden_blocks))
    moment_one_new = 0.9 * moment_one + 0.1 * grad
    moment_two_new = 0.95 * moment_two + 0.05 * grad * grad
    first = moment_one_new / (1.0 - 0.9 ** 20)
    second = moment_two_new / (1.0 - 0.95 ** 20)
    master_new = master - 0.01 * (first / (jnp.sqrt(second) + 1e-08) + 0.1 * master)
    return (master_new, moment_one_new, moment_two_new, master_new.astype(jnp.bfloat16))
```

```python
import functools

import jax
import jax.numpy as jnp
from jax import lax
from jax.experimental import pallas as pl
from jax.experimental.pallas import tpu as pltpu
from jax.sharding import PartitionSpec as P

MESH = pl.DeviceIdType.MESH
GROUP = 4
HID_SLOTS = 4
RECV_SLOTS = 3
EXTRA = 1
FIRST = 1.0 / (1.0 - 0.9**20)
SECOND = 1.0 / (1.0 - 0.95**20)


def kernel(
    n_dp,
    n_ten,
    width,
    gate,
    up,
    cot,
    master,
    one,
    two,
    master_out,
    one_out,
    two_out,
    serving,
    cot_all,
    gates,
    ups,
    hid,
    part,
    inc,
    outg,
    opt_in,
    opt_out,
    served,
    cot_send,
    cot_recv,
    fwd_send,
    fwd_recv,
    own_sem,
    act_sem,
    hid_send,
    hid_recv,
    hid_free,
    sum_send,
    sum_recv,
    sum_free,
    opt_sem,
    res_sem,
    srv_send,
    srv_recv,
    srv_own,
):
    tokens, hidden_cols = gate.shape
    rows = master.shape[0]
    n = hidden_cols // width
    ranks = n_dp // GROUP
    per = ranks // n_ten
    part_slots = part.shape[0]
    last = ranks - 1

    me = lax.axis_index("dp")
    ten = lax.axis_index("tensor")
    rank = lax.div(me, GROUP)
    g = lax.rem(me, GROUP)
    sib = me + 1 - 2 * lax.rem(g, 2)
    far = me + 2 - 4 * lax.div(g, 2)
    g_far = g + 2 - 4 * lax.div(g, 2)
    peers = [rank * GROUP + lax.rem(g + d, GROUP) for d in range(1, GROUP)]
    partners = [lax.rem(ten + d, n_ten) for d in range(1, n_ten)]
    below = me - GROUP
    above = me + GROUP

    barrier = pltpu.get_barrier_semaphore()
    for peer in peers:
        pl.semaphore_signal(barrier, inc=1, device_id=(peer, ten), device_id_type=MESH)
    for partner in partners:
        pl.semaphore_signal(barrier, inc=1, device_id=(me, partner), device_id_type=MESH)
    for step in (1, ranks - 1):
        other = lax.rem(rank + step, ranks) * GROUP + g
        pl.semaphore_signal(barrier, inc=1, device_id=(other, ten), device_id_type=MESH)
    pl.semaphore_wait(barrier, len(peers) + len(partners) + 2)

    def cols(k):
        return pl.ds(pl.multiple_of(k * width, width), width)

    def toks(who):
        return pl.ds(pl.multiple_of(who * tokens, tokens), tokens)

    def remote(src, dst, send, recv, dp, tensor):
        return pltpu.make_async_remote_copy(
            src_ref=src,
            dst_ref=dst,
            send_sem=send,
            recv_sem=recv,
            device_id=(dp, tensor),
            device_id_type=MESH,
        )

    def cot_here(who):
        return cot_all.at[pl.ds(ten * per, per), :, toks(who)]

    def cot_out(d):
        to = lax.rem(g + d, GROUP)
        return remote(
            cot.at[:, to], cot_here(g), cot_send.at[d - 1], cot_recv.at[d - 1],
            rank * GROUP + to, ten,
        )

    def cot_fwd(d, e):
        src = cot.at[:, g] if d == 0 else cot_here(lax.rem(g + GROUP - d, GROUP))
        return remote(
            src, cot_here(lax.rem(g + GROUP - d, GROUP)),
            fwd_send.at[e - 1, d], fwd_recv.at[e - 1, d], me, lax.rem(ten + e, n_ten),
        )

    def own_cot():
        return pltpu.make_async_copy(cot.at[:, g], cot_here(g), own_sem)

    def acts(k):
        s = lax.rem(k, 2)
        return (
            pltpu.make_async_copy(gate.at[:, cols(k)], gates.at[s], act_sem.at[0, s]),
            pltpu.make_async_copy(up.at[:, cols(k)], ups.at[s], act_sem.at[1, s]),
        )

    def opts(k):
        s = lax.rem(k, 2)
        return [
            pltpu.make_async_copy(ref.at[:, cols(k)], opt_in.at[s, j], opt_sem.at[j, s])
            for j, ref in enumerate((master, one, two))
        ]

    def results(k):
        s = lax.rem(k, 2)
        return [
            pltpu.make_async_copy(opt_out.at[s, j], ref.at[:, cols(k)], res_sem.at[j, s])
            for j, ref in enumerate((master_out, one_out, two_out))
        ]

    def hid_copy(k, which):
        s = lax.rem(k, HID_SLOTS)
        block = hid.at[s, toks(g_far if which == 2 else g)]
        to = far if which == 1 else sib
        return remote(block, block, hid_send.at[which, s], hid_recv.at[which, s], to, ten)

    def sum_copy(k, way, t):
        s = lax.rem(k, 2)
        e = lax.rem(k, RECV_SLOTS)
        return remote(
            outg.at[way, s, t], inc.at[way, e, t], sum_send.at[way, s, t],
            sum_recv.at[way, e, t], above if way == 0 else below, ten,
        )

    def srv_cols(k):
        start = ten * hidden_cols + k * width
        return pl.ds(pl.multiple_of(start, width), width)

    def srv_local(k):
        s = lax.rem(k, 2)
        return pltpu.make_async_copy(served.at[s, ten], serving.at[:, srv_cols(k)], srv_own.at[s])

    def srv_copy(k, d):
        s = lax.rem(k, 2)
        to = lax.rem(ten + d, n_ten)
        return remote(
            served.at[s, to], serving.at[:, srv_cols(k)], srv_send.at[d - 1, s],
            srv_recv.at[d - 1], me, to,
        )

    for d in range(1, GROUP):
        cot_out(d).start()
    for e in range(1, n_ten):
        cot_fwd(0, e).start()
    own_cot().start()
    for copy in acts(0):
        copy.start()
    for copy in opts(0):
        copy.start()

    def step(i, carry):
        @pl.when(i < n)
        def _():
            s = lax.rem(i, HID_SLOTS)
            q = lax.rem(i, 2)
            for copy in acts(i):
                copy.wait()

            @pl.when(i + 1 < n)
            def _():
                for copy in acts(i + 1):
                    copy.start()

            def rows_of(j, c):
                piece = pl.ds(pl.multiple_of(j * 64, 64), 64)
                v = gates[q, piece].astype(jnp.float32)
                u = ups[q, piece].astype(jnp.float32)
                value = (0.5 * v) * (1.0 + jnp.tanh(0.5 * v)) * u
                place = pl.ds(pl.multiple_of(g * tokens + j * 64, 64), 64)
                hid[s, place] = value.astype(jnp.bfloat16)
                return c

            lax.fori_loop(0, tokens // 64, rows_of, 0)

            @pl.when(i >= HID_SLOTS)
            def _():
                pl.semaphore_wait(hid_free.at[0], 1)
                pl.semaphore_wait(hid_free.at[1], 1)

            hid_copy(i, 1).start()
            hid_copy(i, 0).start()

        @pl.when(i == 0)
        def _():
            for d in range(1, GROUP):
                cot_out(d).wait_recv()
                for e in range(1, n_ten):
                    cot_fwd(d, e).start()

        b = i - 1

        @pl.when((b >= 0) & (b < n))
        def _():
            hid_copy(b, 1).wait_recv()
            hid_copy(b, 2).start()

        c = i - 2

        @pl.when(c == 0)
        def _():
            own_cot().wait()
            for d in range(GROUP):
                for e in range(1, n_ten):
                    cot_fwd(d, e).wait()
            for d in range(1, GROUP):
                cot_out(d).wait_send()

        @pl.when((c >= 0) & (c < n))
        def _():
            s = lax.rem(c, HID_SLOTS)
            hid_copy(c, 0).wait_recv()
            hid_copy(c, 2).wait_recv()

            def product(t, carry):
                part[lax.rem(c, part_slots), t] = jnp.dot(
                    cot_all[t], hid[s], preferred_element_type=jnp.float32
                )
                return carry

            lax.fori_loop(0, ranks, product, 0)
            for which in range(3):
                hid_copy(c, which).wait_send()

            @pl.when(c + HID_SLOTS < n)
            def _():
                pl.semaphore_signal(
                    hid_free.at[0], inc=1, device_id=(sib, ten), device_id_type=MESH
                )
                pl.semaphore_signal(
                    hid_free.at[1], inc=1, device_id=(far, ten), device_id_type=MESH
                )

        for way in (0, 1):
            hops = rank if way == 0 else last - rank
            k = i - 2 - hops
            source = below if way == 0 else above

            @pl.when((k >= 0) & (k < n))
            def _(way=way, hops=hops, k=k, source=source):
                ps = lax.rem(k, part_slots)
                es = lax.rem(k, RECV_SLOTS)
                qs = lax.rem(k, 2)

                def one_target(t, carry):
                    ahead = (t > rank) if way == 0 else (t < rank)

                    @pl.when((hops > 0) & (ahead | (t == rank)))
                    def _():
                        sum_copy(k, way, t).wait_recv()

                    @pl.when(ahead)
                    def _():
                        @pl.when(k >= 2)
                        def _():
                            sum_copy(k, way, t).wait_send()

                        @pl.when(hops > 0)
                        def _():
                            def rows_of(j, c):
                                piece = pl.ds(pl.multiple_of(j * 32, 32), 32)
                                value = part[ps, t, piece] + inc[way, es, t, piece].astype(
                                    jnp.float32
                                )
                                outg[way, qs, t, piece] = value.astype(jnp.bfloat16)
                                return c

                            lax.fori_loop(0, rows // 32, rows_of, 0)

                        @pl.when(hops == 0)
                        def _():
                            def rows_of(j, c):
                                piece = pl.ds(pl.multiple_of(j * 32, 32), 32)
                                outg[way, qs, t, piece] = part[ps, t, piece].astype(jnp.bfloat16)
                                return c

                            lax.fori_loop(0, rows // 32, rows_of, 0)

                        @pl.when(k >= RECV_SLOTS)
                        def _():
                            pl.semaphore_wait(sum_free.at[way, t], 1)

                        sum_copy(k, way, t).start()

                    @pl.when((hops > 0) & (t == rank))
                    def _():
                        def rows_of(j, c):
                            piece = pl.ds(pl.multiple_of(j * 32, 32), 32)
                            part[ps, t, piece] += inc[way, es, t, piece].astype(jnp.float32)
                            return c

                        lax.fori_loop(0, rows // 32, rows_of, 0)

                    @pl.when((hops > 0) & (ahead | (t == rank)) & (k + RECV_SLOTS < n))
                    def _():
                        pl.semaphore_signal(
                            sum_free.at[way, t], inc=1, device_id=(source, ten),
                            device_id_type=MESH,
                        )

                    return carry

                lax.fori_loop(0, ranks, one_target, 0)

        f = i - 2 - last - EXTRA

        @pl.when((f >= 0) & (f < n))
        def _():
            ps = lax.rem(f, part_slots)
            s = lax.rem(f, 2)
            for copy in opts(f):
                copy.wait()

            @pl.when(f + 1 < n)
            def _():
                for copy in opts(f + 1):
                    copy.start()

            @pl.when(f >= 2)
            def _():
                for copy in results(f):
                    copy.wait()
                srv_local(f).wait()
                for d in range(1, n_ten):
                    srv_copy(f, d).wait_send()

            def rows_of(j, c):
                piece = pl.ds(pl.multiple_of(j * 32, 32), 32)
                grad = part[ps, rank, piece]
                m = 0.9 * opt_in[s, 1, piece] + 0.1 * grad
                v = 0.95 * opt_in[s, 2, piece] + 0.05 * grad * grad
                old = opt_in[s, 0, piece]
                new = old - 0.01 * ((m * FIRST) / (jnp.sqrt(v * SECOND) + 1e-08) + 0.1 * old)
                opt_out[s, 0, piece] = new
                opt_out[s, 1, piece] = m
                opt_out[s, 2, piece] = v
                return c

            lax.fori_loop(0, rows // 32, rows_of, 0)
            block = rows // n_ten
            for t in range(n_ten):
                served[s, t] = opt_out[s, 0, t * block : (t + 1) * block].astype(jnp.bfloat16)
            for d in range(1, n_ten):
                srv_copy(f, d).start()
            srv_local(f).start()
            for copy in results(f):
                copy.start()

        return carry

    lax.fori_loop(0, n + 2 + last + EXTRA, step, 0)

    for k in range(max(n - 2, 0), n):
        for copy in results(k):
            copy.wait()
        srv_local(k).wait()
        for d in range(1, n_ten):
            srv_copy(k, d).wait_send()
        for way in (0, 1):
            def drain(t, carry, way=way, k=k):
                @pl.when((t > rank) if way == 0 else (t < rank))
                def _():
                    sum_copy(k, way, t).wait_send()

                return carry

            lax.fori_loop(0, ranks, drain, 0)
    for d in range(1, n_ten):
        origin = lax.rem(ten + n_ten - d, n_ten)
        area = serving.at[
            :, pl.ds(pl.multiple_of(origin * hidden_cols, hidden_cols), hidden_cols)
        ]
        remote(area, area, srv_send.at[d - 1, 0], srv_recv.at[d - 1], me, origin).wait_recv()


def on_device(n_dp, n_ten, gate_pre, up_pre, out_grad, master, moment_one, moment_two):
    tokens, hidden_cols = gate_pre.shape
    rows = master.shape[0]
    width = 256 if hidden_cols % 256 == 0 else 128
    ranks = n_dp // GROUP
    per = ranks // n_ten
    cot = out_grad.T.reshape(per, GROUP, rows, tokens)
    part_slots = ranks + EXTRA
    f32, bf16 = jnp.float32, jnp.bfloat16
    DMA, REG = pltpu.SemaphoreType.DMA, pltpu.SemaphoreType.REGULAR
    scratch = [
        pltpu.VMEM((ranks, rows, GROUP * tokens), bf16),
        pltpu.VMEM((2, tokens, width), bf16),
        pltpu.VMEM((2, tokens, width), bf16),
        pltpu.VMEM((HID_SLOTS, GROUP * tokens, width), bf16),
        pltpu.VMEM((part_slots, ranks, rows, width), f32),
        pltpu.VMEM((2, RECV_SLOTS, ranks, rows, width), bf16),
        pltpu.VMEM((2, 2, ranks, rows, width), bf16),
        pltpu.VMEM((2, 3, rows, width), f32),
        pltpu.VMEM((2, 3, rows, width), f32),
        pltpu.VMEM((2, n_ten, rows // n_ten, width), bf16),
        DMA((GROUP - 1,)),
        DMA((GROUP - 1,)),
        DMA((n_ten - 1, GROUP)),
        DMA((n_ten - 1, GROUP)),
        DMA,
        DMA((2, 2)),
        DMA((3, HID_SLOTS)),
        DMA((3, HID_SLOTS)),
        REG((2,)),
        DMA((2, 2, ranks)),
        DMA((2, RECV_SLOTS, ranks)),
        REG((2, ranks)),
        DMA((3, 2)),
        DMA((3, 2)),
        DMA((n_ten - 1, 2)),
        DMA((n_ten - 1,)),
        DMA((2,)),
    ]
    whole = jax.ShapeDtypeStruct((rows, hidden_cols), f32)
    return pl.pallas_call(
        functools.partial(kernel, n_dp, n_ten, width),
        out_shape=(
            whole,
            whole,
            whole,
            jax.ShapeDtypeStruct((rows // n_ten, n_ten * hidden_cols), bf16),
        ),
        in_specs=[pl.BlockSpec(memory_space=pl.ANY)] * 6,
        out_specs=[pl.BlockSpec(memory_space=pl.ANY)] * 4,
        scratch_shapes=scratch,
        compiler_params=pltpu.CompilerParams(
            collective_id=0, has_side_effects=True, vmem_limit_bytes=56 * 2**20
        ),
        cost_estimate=pl.CostEstimate(
            flops=2 * rows * ranks * GROUP * tokens * hidden_cols,
            bytes_accessed=24 * rows * hidden_cols + 4 * tokens * hidden_cols,
            transcendentals=tokens * hidden_cols,
        ),
        name="grad_update",
    )(gate_pre, up_pre, cot, master, moment_one, moment_two)


def solution(mesh):
    placed = (P("dp", "tensor"),) * 6
    return jax.shard_map(
        functools.partial(on_device, mesh.shape["dp"], mesh.shape["tensor"]),
        mesh=mesh,
        in_specs=placed,
        out_specs=(
            P("dp", "tensor"),
            P("dp", "tensor"),
            P("dp", "tensor"),
            P(("dp", "tensor"), None),
        ),
        check_vma=False,
    )
```

```python
import functools

import jax
import jax.numpy as jnp
from jax import lax
from jax.experimental import pallas as pl
from jax.experimental.pallas import tpu as pltpu
from jax.sharding import PartitionSpec as P

MESH = pl.DeviceIdType.MESH
GROUP = 4
LATE = 6
HID_SLOTS = 4 + LATE
RECV_SLOTS = 3
EXTRA = 1
FIRST = 1.0 / (1.0 - 0.9**20)
SECOND = 1.0 / (1.0 - 0.95**20)


def kernel(
    n_dp,
    n_ten,
    width,
    gate,
    up,
    cot,
    master,
    one,
    two,
    master_out,
    one_out,
    two_out,
    serving,
    cot_all,
    gates,
    ups,
    hid,
    part,
    inc,
    outg,
    opt_in,
    opt_out,
    served,
    cot_send,
    cot_recv,
    fwd_send,
    fwd_recv,
    own_sem,
    act_sem,
    hid_send,
    hid_recv,
    hid_free,
    sum_send,
    sum_recv,
    sum_free,
    opt_sem,
    res_sem,
    srv_send,
    srv_recv,
    srv_own,
):
    tokens, hidden_cols = gate.shape
    rows = master.shape[0]
    n = hidden_cols // width
    ranks = n_dp // GROUP
    per = ranks // n_ten
    part_slots = part.shape[0]
    last = ranks - 1

    me = lax.axis_index("dp")
    ten = lax.axis_index("tensor")
    rank = lax.div(me, GROUP)
    g = lax.rem(me, GROUP)
    sib = me + 1 - 2 * lax.rem(g, 2)
    far = me + 2 - 4 * lax.div(g, 2)
    g_far = g + 2 - 4 * lax.div(g, 2)
    peers = [rank * GROUP + lax.rem(g + d, GROUP) for d in range(1, GROUP)]
    partners = [lax.rem(ten + d, n_ten) for d in range(1, n_ten)]
    below = me - GROUP
    above = me + GROUP

    barrier = pltpu.get_barrier_semaphore()
    for peer in peers:
        pl.semaphore_signal(barrier, inc=1, device_id=(peer, ten), device_id_type=MESH)
    for partner in partners:
        pl.semaphore_signal(barrier, inc=1, device_id=(me, partner), device_id_type=MESH)
    for step in (1, ranks - 1):
        other = lax.rem(rank + step, ranks) * GROUP + g
        pl.semaphore_signal(barrier, inc=1, device_id=(other, ten), device_id_type=MESH)
    pl.semaphore_wait(barrier, len(peers) + len(partners) + 2)

    def lag(t):
        return jnp.where(lax.div(t, per) == ten, 0, LATE)

    def cols(k):
        return pl.ds(pl.multiple_of(k * width, width), width)

    def toks(who):
        return pl.ds(pl.multiple_of(who * tokens, tokens), tokens)

    def remote(src, dst, send, recv, dp, tensor):
        return pltpu.make_async_remote_copy(
            src_ref=src,
            dst_ref=dst,
            send_sem=send,
            recv_sem=recv,
            device_id=(dp, tensor),
            device_id_type=MESH,
        )

    def cot_here(who):
        return cot_all.at[pl.ds(ten * per, per), :, toks(who)]

    def cot_out(d):
        to = lax.rem(g + d, GROUP)
        return remote(
            cot.at[:, to], cot_here(g), cot_send.at[d - 1], cot_recv.at[d - 1],
            rank * GROUP + to, ten,
        )

    def cot_fwd(d, e):
        src = cot.at[:, g] if d == 0 else cot_here(lax.rem(g + GROUP - d, GROUP))
        return remote(
            src, cot_here(lax.rem(g + GROUP - d, GROUP)),
            fwd_send.at[e - 1, d], fwd_recv.at[e - 1, d], me, lax.rem(ten + e, n_ten),
        )

    def own_cot():
        return pltpu.make_async_copy(cot.at[:, g], cot_here(g), own_sem)

    def acts(k):
        s = lax.rem(k, 2)
        return (
            pltpu.make_async_copy(gate.at[:, cols(k)], gates.at[s], act_sem.at[0, s]),
            pltpu.make_async_copy(up.at[:, cols(k)], ups.at[s], act_sem.at[1, s]),
        )

    def opts(k):
        s = lax.rem(k, 2)
        return [
            pltpu.make_async_copy(ref.at[:, cols(k)], opt_in.at[s, j], opt_sem.at[j, s])
            for j, ref in enumerate((master, one, two))
        ]

    def results(k):
        s = lax.rem(k, 2)
        return [
            pltpu.make_async_copy(opt_out.at[s, j], ref.at[:, cols(k)], res_sem.at[j, s])
            for j, ref in enumerate((master_out, one_out, two_out))
        ]

    def hid_copy(k, which):
        s = lax.rem(k, HID_SLOTS)
        block = hid.at[s, toks(g_far if which == 2 else g)]
        to = far if which == 1 else sib
        return remote(block, block, hid_send.at[which, s], hid_recv.at[which, s], to, ten)

    def sum_copy(k, way, t):
        s = lax.rem(k, 2)
        e = lax.rem(k, RECV_SLOTS)
        return remote(
            outg.at[way, s, t], inc.at[way, e, t], sum_send.at[way, s, t],
            sum_recv.at[way, e, t], above if way == 0 else below, ten,
        )

    def srv_cols(k):
        start = ten * hidden_cols + k * width
        return pl.ds(pl.multiple_of(start, width), width)

    def srv_local(k):
        s = lax.rem(k, 2)
        return pltpu.make_async_copy(served.at[s, ten], serving.at[:, srv_cols(k)], srv_own.at[s])

    def srv_copy(k, d):
        s = lax.rem(k, 2)
        to = lax.rem(ten + d, n_ten)
        return remote(
            served.at[s, to], serving.at[:, srv_cols(k)], srv_send.at[d - 1, s],
            srv_recv.at[d - 1], me, to,
        )

    for d in range(1, GROUP):
        cot_out(d).start()
    for e in range(1, n_ten):
        cot_fwd(0, e).start()
    own_cot().start()
    for copy in acts(0):
        copy.start()
    for copy in opts(0):
        copy.start()

    def step(i, carry):
        @pl.when(i < n)
        def _():
            s = lax.rem(i, HID_SLOTS)
            q = lax.rem(i, 2)
            for copy in acts(i):
                copy.wait()

            @pl.when(i + 1 < n)
            def _():
                for copy in acts(i + 1):
                    copy.start()

            def rows_of(j, c):
                piece = pl.ds(pl.multiple_of(j * 64, 64), 64)
                v = gates[q, piece].astype(jnp.float32)
                u = ups[q, piece].astype(jnp.float32)
                value = (0.5 * v) * (1.0 + jnp.tanh(0.5 * v)) * u
                place = pl.ds(pl.multiple_of(g * tokens + j * 64, 64), 64)
                hid[s, place] = value.astype(jnp.bfloat16)
                return c

            lax.fori_loop(0, tokens // 64, rows_of, 0)

            @pl.when(i >= HID_SLOTS)
            def _():
                pl.semaphore_wait(hid_free.at[0], 1)
                pl.semaphore_wait(hid_free.at[1], 1)

            hid_copy(i, 1).start()
            hid_copy(i, 0).start()

        @pl.when(i == 0)
        def _():
            for d in range(1, GROUP):
                cot_out(d).wait_recv()
                for e in range(1, n_ten):
                    cot_fwd(d, e).start()

        b = i - 1

        @pl.when((b >= 0) & (b < n))
        def _():
            hid_copy(b, 1).wait_recv()
            hid_copy(b, 2).start()

        c = i - 2

        @pl.when(c == 0)
        def _():
            own_cot().wait()
            for d in range(1, GROUP):
                cot_out(d).wait_send()

        @pl.when(c == LATE)
        def _():
            for d in range(GROUP):
                for e in range(1, n_ten):
                    cot_fwd(d, e).wait()

        @pl.when((c >= 0) & (c < n))
        def _():
            s = lax.rem(c, HID_SLOTS)
            hid_copy(c, 0).wait_recv()
            hid_copy(c, 2).wait_recv()

            for which in range(3):
                hid_copy(c, which).wait_send()

        def product(t, carry):
            k = c - lag(t)

            @pl.when((k >= 0) & (k < n))
            def _():
                part[lax.rem(k, part_slots), t] = jnp.dot(
                    cot_all[t], hid[lax.rem(k, HID_SLOTS)], preferred_element_type=jnp.float32
                )

            return carry

        lax.fori_loop(0, ranks, product, 0)

        @pl.when((c >= LATE) & (c - LATE + HID_SLOTS < n))
        def _():
            pl.semaphore_signal(
                hid_free.at[0], inc=1, device_id=(sib, ten), device_id_type=MESH
            )
            pl.semaphore_signal(
                hid_free.at[1], inc=1, device_id=(far, ten), device_id_type=MESH
            )

        for way in (0, 1):
            hops = rank if way == 0 else last - rank
            source = below if way == 0 else above

            def one_target(t, carry, way=way, hops=hops, source=source):
                k = i - 2 - hops - lag(t)
                ahead = (t > rank) if way == 0 else (t < rank)

                @pl.when((k >= 0) & (k < n) & (ahead | ((t == rank) & (hops > 0))))
                def _():
                    ps = lax.rem(k, part_slots)
                    es = lax.rem(k, RECV_SLOTS)
                    qs = lax.rem(k, 2)

                    @pl.when(hops > 0)
                    def _():
                        sum_copy(k, way, t).wait_recv()

                    @pl.when(ahead)
                    def _():
                        @pl.when(k >= 2)
                        def _():
                            sum_copy(k, way, t).wait_send()

                        @pl.when(hops > 0)
                        def _():
                            def rows_of(j, c):
                                piece = pl.ds(pl.multiple_of(j * 32, 32), 32)
                                value = part[ps, t, piece] + inc[way, es, t, piece].astype(
                                    jnp.float32
                                )
                                outg[way, qs, t, piece] = value.astype(jnp.bfloat16)
                                return c

                            lax.fori_loop(0, rows // 32, rows_of, 0)

                        @pl.when(hops == 0)
                        def _():
                            def rows_of(j, c):
                                piece = pl.ds(pl.multiple_of(j * 32, 32), 32)
                                outg[way, qs, t, piece] = part[ps, t, piece].astype(jnp.bfloat16)
                                return c

                            lax.fori_loop(0, rows // 32, rows_of, 0)

                        @pl.when(k >= RECV_SLOTS)
                        def _():
                            pl.semaphore_wait(sum_free.at[way, t], 1)

                        sum_copy(k, way, t).start()

                    @pl.when(t == rank)
                    def _():
                        def rows_of(j, c):
                            piece = pl.ds(pl.multiple_of(j * 32, 32), 32)
                            part[ps, t, piece] += inc[way, es, t, piece].astype(jnp.float32)
                            return c

                        lax.fori_loop(0, rows // 32, rows_of, 0)

                    @pl.when((hops > 0) & (k + RECV_SLOTS < n))
                    def _():
                        pl.semaphore_signal(
                            sum_free.at[way, t], inc=1, device_id=(source, ten),
                            device_id_type=MESH,
                        )

                return carry

            lax.fori_loop(0, ranks, one_target, 0)

        f = i - 2 - last - EXTRA - lag(rank)

        @pl.when((f >= 0) & (f < n))
        def _():
            ps = lax.rem(f, part_slots)
            s = lax.rem(f, 2)
            for copy in opts(f):
                copy.wait()

            @pl.when(f + 1 < n)
            def _():
                for copy in opts(f + 1):
                    copy.start()

            @pl.when(f >= 2)
            def _():
                for copy in results(f):
                    copy.wait()
                srv_local(f).wait()
                for d in range(1, n_ten):
                    srv_copy(f, d).wait_send()

            def rows_of(j, c):
                piece = pl.ds(pl.multiple_of(j * 32, 32), 32)
                grad = part[ps, rank, piece]
                m = 0.9 * opt_in[s, 1, piece] + 0.1 * grad
                v = 0.95 * opt_in[s, 2, piece] + 0.05 * grad * grad
                old = opt_in[s, 0, piece]
                new = old - 0.01 * ((m * FIRST) / (jnp.sqrt(v * SECOND) + 1e-08) + 0.1 * old)
                opt_out[s, 0, piece] = new
                opt_out[s, 1, piece] = m
                opt_out[s, 2, piece] = v
                return c

            lax.fori_loop(0, rows // 32, rows_of, 0)
            block = rows // n_ten
            for t in range(n_ten):
                served[s, t] = opt_out[s, 0, t * block : (t + 1) * block].astype(jnp.bfloat16)
            for d in range(1, n_ten):
                srv_copy(f, d).start()
            srv_local(f).start()
            for copy in results(f):
                copy.start()

        return carry

    lax.fori_loop(0, n + 2 + last + EXTRA + LATE, step, 0)

    for k in range(max(n - 2, 0), n):
        for copy in results(k):
            copy.wait()
        srv_local(k).wait()
        for d in range(1, n_ten):
            srv_copy(k, d).wait_send()
        for way in (0, 1):
            def drain(t, carry, way=way, k=k):
                @pl.when((t > rank) if way == 0 else (t < rank))
                def _():
                    sum_copy(k, way, t).wait_send()

                return carry

            lax.fori_loop(0, ranks, drain, 0)
    for d in range(1, n_ten):
        origin = lax.rem(ten + n_ten - d, n_ten)
        area = serving.at[
            :, pl.ds(pl.multiple_of(origin * hidden_cols, hidden_cols), hidden_cols)
        ]
        remote(area, area, srv_send.at[d - 1, 0], srv_recv.at[d - 1], me, origin).wait_recv()


def on_device(n_dp, n_ten, gate_pre, up_pre, out_grad, master, moment_one, moment_two):
    tokens, hidden_cols = gate_pre.shape
    rows = master.shape[0]
    width = 256 if hidden_cols % 256 == 0 else 128
    ranks = n_dp // GROUP
    per = ranks // n_ten
    cot = out_grad.T.reshape(per, GROUP, rows, tokens)
    part_slots = ranks + EXTRA
    f32, bf16 = jnp.float32, jnp.bfloat16
    DMA, REG = pltpu.SemaphoreType.DMA, pltpu.SemaphoreType.REGULAR
    scratch = [
        pltpu.VMEM((ranks, rows, GROUP * tokens), bf16),
        pltpu.VMEM((2, tokens, width), bf16),
        pltpu.VMEM((2, tokens, width), bf16),
        pltpu.VMEM((HID_SLOTS, GROUP * tokens, width), bf16),
        pltpu.VMEM((part_slots, ranks, rows, width), f32),
        pltpu.VMEM((2, RECV_SLOTS, ranks, rows, width), bf16),
        pltpu.VMEM((2, 2, ranks, rows, width), bf16),
        pltpu.VMEM((2, 3, rows, width), f32),
        pltpu.VMEM((2, 3, rows, width), f32),
        pltpu.VMEM((2, n_ten, rows // n_ten, width), bf16),
        DMA((GROUP - 1,)),
        DMA((GROUP - 1,)),
        DMA((n_ten - 1, GROUP)),
        DMA((n_ten - 1, GROUP)),
        DMA,
        DMA((2, 2)),
        DMA((3, HID_SLOTS)),
        DMA((3, HID_SLOTS)),
        REG((2,)),
        DMA((2, 2, ranks)),
        DMA((2, RECV_SLOTS, ranks)),
        REG((2, ranks)),
        DMA((3, 2)),
        DMA((3, 2)),
        DMA((n_ten - 1, 2)),
        DMA((n_ten - 1,)),
        DMA((2,)),
    ]
    whole = jax.ShapeDtypeStruct((rows, hidden_cols), f32)
    return pl.pallas_call(
        functools.partial(kernel, n_dp, n_ten, width),
        out_shape=(
            whole,
            whole,
            whole,
            jax.ShapeDtypeStruct((rows // n_ten, n_ten * hidden_cols), bf16),
        ),
        in_specs=[pl.BlockSpec(memory_space=pl.ANY)] * 6,
        out_specs=[pl.BlockSpec(memory_space=pl.ANY)] * 4,
        scratch_shapes=scratch,
        compiler_params=pltpu.CompilerParams(
            collective_id=0, has_side_effects=True, vmem_limit_bytes=56 * 2**20
        ),
        cost_estimate=pl.CostEstimate(
            flops=2 * rows * ranks * GROUP * tokens * hidden_cols,
            bytes_accessed=24 * rows * hidden_cols + 4 * tokens * hidden_cols,
            transcendentals=tokens * hidden_cols,
        ),
        name="grad_update",
    )(gate_pre, up_pre, cot, master, moment_one, moment_two)


def solution(mesh):
    placed = (P("dp", "tensor"),) * 6
    return jax.shard_map(
        functools.partial(on_device, mesh.shape["dp"], mesh.shape["tensor"]),
        mesh=mesh,
        in_specs=placed,
        out_specs=(
            P("dp", "tensor"),
            P("dp", "tensor"),
            P("dp", "tensor"),
            P(("dp", "tensor"), None),
        ),
        check_vma=False,
    )
```

```python
import functools

import jax
import jax.numpy as jnp
from jax import lax
from jax.experimental import pallas as pl
from jax.experimental.pallas import tpu as pltpu
from jax.sharding import PartitionSpec as P

MESH = pl.DeviceIdType.MESH
GROUP = 4
LATE = 4
HID_SLOTS = 4 + LATE
RECV_SLOTS = 3
EXTRA = 1
FIRST = 1.0 / (1.0 - 0.9**20)
SECOND = 1.0 / (1.0 - 0.95**20)


def kernel(
    n_dp,
    n_ten,
    width,
    gate,
    up,
    cot,
    master,
    one,
    two,
    master_out,
    one_out,
    two_out,
    serving,
    cot_all,
    gates,
    ups,
    hid,
    part,
    inc,
    outg,
    opt_in,
    opt_out,
    served,
    cot_send,
    cot_recv,
    fwd_send,
    fwd_recv,
    own_sem,
    act_sem,
    hid_send,
    hid_recv,
    hid_free,
    sum_send,
    sum_recv,
    sum_free,
    opt_sem,
    res_sem,
    srv_send,
    srv_recv,
    srv_own,
):
    tokens, hidden_cols = gate.shape
    rows = master.shape[0]
    n = hidden_cols // width
    ranks = n_dp // GROUP
    per = ranks // n_ten
    part_slots = part.shape[0]
    last = ranks - 1

    me = lax.axis_index("dp")
    ten = lax.axis_index("tensor")
    rank = lax.div(me, GROUP)
    g = lax.rem(me, GROUP)
    sib = me + 1 - 2 * lax.rem(g, 2)
    far = me + 2 - 4 * lax.div(g, 2)
    g_far = g + 2 - 4 * lax.div(g, 2)
    peers = [rank * GROUP + lax.rem(g + d, GROUP) for d in range(1, GROUP)]
    partners = [lax.rem(ten + d, n_ten) for d in range(1, n_ten)]
    below = me - GROUP
    above = me + GROUP

    barrier = pltpu.get_barrier_semaphore()
    for peer in peers:
        pl.semaphore_signal(barrier, inc=1, device_id=(peer, ten), device_id_type=MESH)
    for partner in partners:
        pl.semaphore_signal(barrier, inc=1, device_id=(me, partner), device_id_type=MESH)
    for step in (1, ranks - 1):
        other = lax.rem(rank + step, ranks) * GROUP + g
        pl.semaphore_signal(barrier, inc=1, device_id=(other, ten), device_id_type=MESH)
    pl.semaphore_wait(barrier, len(peers) + len(partners) + 2)

    def lag(t):
        return jnp.where(lax.div(t, per) == ten, 0, LATE)

    big, small = rows // 2, rows // 5

    def here(t, j, size):
        return pl.ds(pl.multiple_of(t * rows + j * size, 16), size)

    def cols(k):
        return pl.ds(pl.multiple_of(k * width, width), width)

    def toks(who):
        return pl.ds(pl.multiple_of(who * tokens, tokens), tokens)

    def remote(src, dst, send, recv, dp, tensor):
        return pltpu.make_async_remote_copy(
            src_ref=src,
            dst_ref=dst,
            send_sem=send,
            recv_sem=recv,
            device_id=(dp, tensor),
            device_id_type=MESH,
        )

    def cot_here(who):
        half = per * rows
        return cot_all.at[pl.ds(pl.multiple_of(ten * half, half), half), toks(who)]

    def cot_out(d):
        to = lax.rem(g + d, GROUP)
        return remote(
            cot.at[to], cot_here(g), cot_send.at[d - 1], cot_recv.at[d - 1],
            rank * GROUP + to, ten,
        )

    def cot_fwd(d, e):
        src = cot.at[g] if d == 0 else cot_here(lax.rem(g + GROUP - d, GROUP))
        return remote(
            src, cot_here(lax.rem(g + GROUP - d, GROUP)),
            fwd_send.at[e - 1, d], fwd_recv.at[e - 1, d], me, lax.rem(ten + e, n_ten),
        )

    def own_cot():
        return pltpu.make_async_copy(cot.at[g], cot_here(g), own_sem)

    def acts(k):
        s = lax.rem(k, 2)
        return (
            pltpu.make_async_copy(gate.at[:, cols(k)], gates.at[s], act_sem.at[0, s]),
            pltpu.make_async_copy(up.at[:, cols(k)], ups.at[s], act_sem.at[1, s]),
        )

    def opts(k):
        s = lax.rem(k, 2)
        return [
            pltpu.make_async_copy(ref.at[:, cols(k)], opt_in.at[s, j], opt_sem.at[j, s])
            for j, ref in enumerate((master, one, two))
        ]

    def results(k):
        s = lax.rem(k, 2)
        return [
            pltpu.make_async_copy(opt_out.at[s, j], ref.at[:, cols(k)], res_sem.at[j, s])
            for j, ref in enumerate((master_out, one_out, two_out))
        ]

    def hid_copy(k, which):
        s = lax.rem(k, HID_SLOTS)
        block = hid.at[s, toks(g_far if which == 2 else g)]
        to = far if which == 1 else sib
        return remote(block, block, hid_send.at[which, s], hid_recv.at[which, s], to, ten)

    def sum_copy(k, way, t):
        s = lax.rem(k, 2)
        e = lax.rem(k, RECV_SLOTS)
        return remote(
            outg.at[way, s, t], inc.at[way, e, t], sum_send.at[way, s, t],
            sum_recv.at[way, e, t], above if way == 0 else below, ten,
        )

    def srv_cols(k):
        start = ten * hidden_cols + k * width
        return pl.ds(pl.multiple_of(start, width), width)

    def srv_local(k):
        s = lax.rem(k, 2)
        return pltpu.make_async_copy(served.at[s, ten], serving.at[:, srv_cols(k)], srv_own.at[s])

    def srv_copy(k, d):
        s = lax.rem(k, 2)
        to = lax.rem(ten + d, n_ten)
        return remote(
            served.at[s, to], serving.at[:, srv_cols(k)], srv_send.at[d - 1, s],
            srv_recv.at[d - 1], me, to,
        )

    for d in range(1, GROUP):
        cot_out(d).start()
    for e in range(1, n_ten):
        cot_fwd(0, e).start()
    own_cot().start()
    for copy in acts(0):
        copy.start()
    for copy in opts(0):
        copy.start()

    def step(i, carry):
        @pl.when(i < n)
        def _():
            s = lax.rem(i, HID_SLOTS)
            q = lax.rem(i, 2)
            for copy in acts(i):
                copy.wait()

            @pl.when(i + 1 < n)
            def _():
                for copy in acts(i + 1):
                    copy.start()

            def rows_of(j, c):
                piece = pl.ds(pl.multiple_of(j * 128, 128), 128)
                v = gates[q, piece].astype(jnp.float32)
                u = ups[q, piece].astype(jnp.float32)
                value = (0.5 * v) * (1.0 + jnp.tanh(0.5 * v)) * u
                place = pl.ds(pl.multiple_of(g * tokens + j * 128, 128), 128)
                hid[s, place] = value.astype(jnp.bfloat16)
                return c

            lax.fori_loop(0, tokens // 128, rows_of, 0)

            @pl.when(i >= HID_SLOTS)
            def _():
                pl.semaphore_wait(hid_free.at[0], 1)
                pl.semaphore_wait(hid_free.at[1], 1)

            hid_copy(i, 1).start()
            hid_copy(i, 0).start()

        @pl.when(i == 0)
        def _():
            for d in range(1, GROUP):
                cot_out(d).wait_recv()
                for e in range(1, n_ten):
                    cot_fwd(d, e).start()

        b = i - 1

        @pl.when((b >= 0) & (b < n))
        def _():
            hid_copy(b, 1).wait_recv()
            hid_copy(b, 2).start()

        c = i - 2

        @pl.when(c == 0)
        def _():
            own_cot().wait()
            for d in range(1, GROUP):
                cot_out(d).wait_send()

        @pl.when(c == LATE)
        def _():
            for d in range(GROUP):
                for e in range(1, n_ten):
                    cot_fwd(d, e).wait()

        @pl.when((c >= 0) & (c < n))
        def _():
            s = lax.rem(c, HID_SLOTS)
            hid_copy(c, 0).wait_recv()
            hid_copy(c, 2).wait_recv()

            for which in range(3):
                hid_copy(c, which).wait_send()

        def product(j, carry):
            k = c - jnp.where(j == ten, 0, LATE)

            @pl.when((k >= 0) & (k < n))
            def _():
                half = per * rows
                place = pl.ds(pl.multiple_of(j * half, half), half)
                part[lax.rem(k, part_slots), place] = jnp.dot(
                    cot_all[place], hid[lax.rem(k, HID_SLOTS)], preferred_element_type=jnp.float32
                )

            return carry

        lax.fori_loop(0, n_ten, product, 0)

        @pl.when((c >= LATE) & (c - LATE + HID_SLOTS < n))
        def _():
            pl.semaphore_signal(
                hid_free.at[0], inc=1, device_id=(sib, ten), device_id_type=MESH
            )
            pl.semaphore_signal(
                hid_free.at[1], inc=1, device_id=(far, ten), device_id_type=MESH
            )

        for way in (0, 1):
            hops = rank if way == 0 else last - rank
            source = below if way == 0 else above

            def one_target(t, carry, way=way, hops=hops, source=source):
                k = i - 2 - hops - lag(t)
                ahead = (t > rank) if way == 0 else (t < rank)

                @pl.when((k >= 0) & (k < n) & (ahead | ((t == rank) & (hops > 0))))
                def _():
                    ps = lax.rem(k, part_slots)
                    es = lax.rem(k, RECV_SLOTS)
                    qs = lax.rem(k, 2)

                    @pl.when(hops > 0)
                    def _():
                        sum_copy(k, way, t).wait_recv()

                    @pl.when(ahead)
                    def _():
                        @pl.when(k >= 2)
                        def _():
                            sum_copy(k, way, t).wait_send()

                        @pl.when(hops > 0)
                        def _():
                            def rows_of(j, c):
                                piece = pl.ds(pl.multiple_of(j * big, big), big)
                                value = part[ps, here(t, j, big)] + inc[way, es, t, piece].astype(
                                    jnp.float32
                                )
                                outg[way, qs, t, piece] = value.astype(jnp.bfloat16)
                                return c

                            lax.fori_loop(0, rows // big, rows_of, 0)

                        @pl.when(hops == 0)
                        def _():
                            def rows_of(j, c):
                                piece = pl.ds(pl.multiple_of(j * big, big), big)
                                outg[way, qs, t, piece] = part[ps, here(t, j, big)].astype(jnp.bfloat16)
                                return c

                            lax.fori_loop(0, rows // big, rows_of, 0)

                        @pl.when(k >= RECV_SLOTS)
                        def _():
                            pl.semaphore_wait(sum_free.at[way, t], 1)

                        sum_copy(k, way, t).start()

                    @pl.when(t == rank)
                    def _():
                        def rows_of(j, c):
                            piece = pl.ds(pl.multiple_of(j * big, big), big)
                            part[ps, here(t, j, big)] += inc[way, es, t, piece].astype(jnp.float32)
                            return c

                        lax.fori_loop(0, rows // big, rows_of, 0)

                    @pl.when((hops > 0) & (k + RECV_SLOTS < n))
                    def _():
                        pl.semaphore_signal(
                            sum_free.at[way, t], inc=1, device_id=(source, ten),
                            device_id_type=MESH,
                        )

                return carry

            lax.fori_loop(0, ranks, one_target, 0)

        f = i - 2 - last - EXTRA - lag(rank)

        @pl.when((f >= 0) & (f < n))
        def _():
            ps = lax.rem(f, part_slots)
            s = lax.rem(f, 2)
            for copy in opts(f):
                copy.wait()

            @pl.when(f + 1 < n)
            def _():
                for copy in opts(f + 1):
                    copy.start()

            @pl.when(f >= 2)
            def _():
                for copy in results(f):
                    copy.wait()
                srv_local(f).wait()
                for d in range(1, n_ten):
                    srv_copy(f, d).wait_send()

            def rows_of(j, c):
                piece = pl.ds(pl.multiple_of(j * small, small), small)
                grad = part[ps, here(rank, j, small)]
                m = 0.9 * opt_in[s, 1, piece] + 0.1 * grad
                v = 0.95 * opt_in[s, 2, piece] + 0.05 * grad * grad
                old = opt_in[s, 0, piece]
                new = old - 0.01 * ((m * FIRST) / (jnp.sqrt(v * SECOND) + 1e-08) + 0.1 * old)
                opt_out[s, 0, piece] = new
                opt_out[s, 1, piece] = m
                opt_out[s, 2, piece] = v
                return c

            lax.fori_loop(0, rows // small, rows_of, 0)
            block = rows // n_ten
            for t in range(n_ten):
                served[s, t] = opt_out[s, 0, t * block : (t + 1) * block].astype(jnp.bfloat16)
            for d in range(1, n_ten):
                srv_copy(f, d).start()
            srv_local(f).start()
            for copy in results(f):
                copy.start()

        return carry

    lax.fori_loop(0, n + 2 + last + EXTRA + LATE, step, 0)

    for k in range(max(n - 2, 0), n):
        for copy in results(k):
            copy.wait()
        srv_local(k).wait()
        for d in range(1, n_ten):
            srv_copy(k, d).wait_send()
        for way in (0, 1):
            def drain(t, carry, way=way, k=k):
                @pl.when((t > rank) if way == 0 else (t < rank))
                def _():
                    sum_copy(k, way, t).wait_send()

                return carry

            lax.fori_loop(0, ranks, drain, 0)
    for d in range(1, n_ten):
        origin = lax.rem(ten + n_ten - d, n_ten)
        area = serving.at[
            :, pl.ds(pl.multiple_of(origin * hidden_cols, hidden_cols), hidden_cols)
        ]
        remote(area, area, srv_send.at[d - 1, 0], srv_recv.at[d - 1], me, origin).wait_recv()


def on_device(n_dp, n_ten, gate_pre, up_pre, out_grad, master, moment_one, moment_two):
    tokens, hidden_cols = gate_pre.shape
    rows = master.shape[0]
    width = 256 if hidden_cols % 256 == 0 else 128
    ranks = n_dp // GROUP
    per = ranks // n_ten
    cot = out_grad.T.reshape(per, GROUP, rows, tokens).swapaxes(0, 1)
    cot = cot.reshape(GROUP, per * rows, tokens)
    part_slots = ranks + EXTRA
    f32, bf16 = jnp.float32, jnp.bfloat16
    DMA, REG = pltpu.SemaphoreType.DMA, pltpu.SemaphoreType.REGULAR
    scratch = [
        pltpu.VMEM((ranks * rows, GROUP * tokens), bf16),
        pltpu.VMEM((2, tokens, width), bf16),
        pltpu.VMEM((2, tokens, width), bf16),
        pltpu.VMEM((HID_SLOTS, GROUP * tokens, width), bf16),
        pltpu.VMEM((part_slots, ranks * rows, width), f32),
        pltpu.VMEM((2, RECV_SLOTS, ranks, rows, width), bf16),
        pltpu.VMEM((2, 2, ranks, rows, width), bf16),
        pltpu.VMEM((2, 3, rows, width), f32),
        pltpu.VMEM((2, 3, rows, width), f32),
        pltpu.VMEM((2, n_ten, rows // n_ten, width), bf16),
        DMA((GROUP - 1,)),
        DMA((GROUP - 1,)),
        DMA((n_ten - 1, GROUP)),
        DMA((n_ten - 1, GROUP)),
        DMA,
        DMA((2, 2)),
        DMA((3, HID_SLOTS)),
        DMA((3, HID_SLOTS)),
        REG((2,)),
        DMA((2, 2, ranks)),
        DMA((2, RECV_SLOTS, ranks)),
        REG((2, ranks)),
        DMA((3, 2)),
        DMA((3, 2)),
        DMA((n_ten - 1, 2)),
        DMA((n_ten - 1,)),
        DMA((2,)),
    ]
    whole = jax.ShapeDtypeStruct((rows, hidden_cols), f32)
    return pl.pallas_call(
        functools.partial(kernel, n_dp, n_ten, width),
        out_shape=(
            whole,
            whole,
            whole,
            jax.ShapeDtypeStruct((rows // n_ten, n_ten * hidden_cols), bf16),
        ),
        in_specs=[pl.BlockSpec(memory_space=pl.ANY)] * 6,
        out_specs=[pl.BlockSpec(memory_space=pl.ANY)] * 4,
        scratch_shapes=scratch,
        compiler_params=pltpu.CompilerParams(
            collective_id=0, has_side_effects=True, vmem_limit_bytes=56 * 2**20
        ),
        cost_estimate=pl.CostEstimate(
            flops=2 * rows * ranks * GROUP * tokens * hidden_cols,
            bytes_accessed=24 * rows * hidden_cols + 4 * tokens * hidden_cols,
            transcendentals=tokens * hidden_cols,
        ),
        name="grad_update",
    )(gate_pre, up_pre, cot, master, moment_one, moment_two)


def solution(mesh):
    placed = (P("dp", "tensor"),) * 6
    return jax.shard_map(
        functools.partial(on_device, mesh.shape["dp"], mesh.shape["tensor"]),
        mesh=mesh,
        in_specs=placed,
        out_specs=(
            P("dp", "tensor"),
            P("dp", "tensor"),
            P("dp", "tensor"),
            P(("dp", "tensor"), None),
        ),
        check_vma=False,
    )
```

```python
import functools

import jax
import jax.numpy as jnp
from jax import lax
from jax.experimental import pallas as pl
from jax.experimental.pallas import tpu as pltpu
from jax.sharding import PartitionSpec as P

MESH = pl.DeviceIdType.MESH
GROUP = 4
LATE = 4
HID_SLOTS = 4 + LATE
RECV_SLOTS = 5
SEND_SLOTS = 3
HOP = 2
EXTRA = 0
FIRST = 1.0 / (1.0 - 0.9**20)
SECOND = 1.0 / (1.0 - 0.95**20)


def kernel(
    n_dp,
    n_ten,
    width,
    gate,
    up,
    cot,
    master,
    one,
    two,
    master_out,
    one_out,
    two_out,
    serving,
    cot_all,
    gates,
    ups,
    hid,
    part,
    inc,
    outg,
    opt_in,
    opt_out,
    served,
    cot_send,
    cot_recv,
    fwd_send,
    fwd_recv,
    own_sem,
    act_sem,
    hid_send,
    hid_recv,
    hid_free,
    sum_send,
    sum_recv,
    sum_free,
    opt_sem,
    res_sem,
    srv_send,
    srv_recv,
    srv_own,
):
    tokens, hidden_cols = gate.shape
    rows = master.shape[0]
    n = hidden_cols // width
    ranks = n_dp // GROUP
    per = ranks // n_ten
    part_slots = part.shape[0]
    last = ranks - 1

    me = lax.axis_index("dp")
    ten = lax.axis_index("tensor")
    rank = lax.div(me, GROUP)
    g = lax.rem(me, GROUP)
    sib = me + 1 - 2 * lax.rem(g, 2)
    far = me + 2 - 4 * lax.div(g, 2)
    g_far = g + 2 - 4 * lax.div(g, 2)
    peers = [rank * GROUP + lax.rem(g + d, GROUP) for d in range(1, GROUP)]
    partners = [lax.rem(ten + d, n_ten) for d in range(1, n_ten)]
    below = me - GROUP
    above = me + GROUP

    barrier = pltpu.get_barrier_semaphore()
    for peer in peers:
        pl.semaphore_signal(barrier, inc=1, device_id=(peer, ten), device_id_type=MESH)
    for partner in partners:
        pl.semaphore_signal(barrier, inc=1, device_id=(me, partner), device_id_type=MESH)
    for step in (1, ranks - 1):
        other = lax.rem(rank + step, ranks) * GROUP + g
        pl.semaphore_signal(barrier, inc=1, device_id=(other, ten), device_id_type=MESH)
    pl.semaphore_wait(barrier, len(peers) + len(partners) + 2)

    def lag(t):
        return jnp.where(lax.div(t, per) == ten, 0, LATE)

    big, small = rows // 2, rows // 5

    def here(t, j, size):
        return pl.ds(pl.multiple_of(t * rows + j * size, 16), size)

    def cols(k):
        return pl.ds(pl.multiple_of(k * width, width), width)

    def toks(who):
        return pl.ds(pl.multiple_of(who * tokens, tokens), tokens)

    def remote(src, dst, send, recv, dp, tensor):
        return pltpu.make_async_remote_copy(
            src_ref=src,
            dst_ref=dst,
            send_sem=send,
            recv_sem=recv,
            device_id=(dp, tensor),
            device_id_type=MESH,
        )

    def cot_here(who):
        half = per * rows
        return cot_all.at[pl.ds(pl.multiple_of(ten * half, half), half), toks(who)]

    def cot_out(d):
        to = lax.rem(g + d, GROUP)
        return remote(
            cot.at[to], cot_here(g), cot_send.at[d - 1], cot_recv.at[d - 1],
            rank * GROUP + to, ten,
        )

    def cot_fwd(d, e):
        src = cot.at[g] if d == 0 else cot_here(lax.rem(g + GROUP - d, GROUP))
        return remote(
            src, cot_here(lax.rem(g + GROUP - d, GROUP)),
            fwd_send.at[e - 1, d], fwd_recv.at[e - 1, d], me, lax.rem(ten + e, n_ten),
        )

    def own_cot():
        return pltpu.make_async_copy(cot.at[g], cot_here(g), own_sem)

    def acts(k):
        s = lax.rem(k, 2)
        return (
            pltpu.make_async_copy(gate.at[:, cols(k)], gates.at[s], act_sem.at[0, s]),
            pltpu.make_async_copy(up.at[:, cols(k)], ups.at[s], act_sem.at[1, s]),
        )

    def opts(k):
        s = lax.rem(k, 2)
        return [
            pltpu.make_async_copy(ref.at[:, cols(k)], opt_in.at[s, j], opt_sem.at[j, s])
            for j, ref in enumerate((master, one, two))
        ]

    def results(k):
        s = lax.rem(k, 2)
        return [
            pltpu.make_async_copy(opt_out.at[s, j], ref.at[:, cols(k)], res_sem.at[j, s])
            for j, ref in enumerate((master_out, one_out, two_out))
        ]

    def hid_copy(k, which):
        s = lax.rem(k, HID_SLOTS)
        block = hid.at[s, toks(g_far if which == 2 else g)]
        to = far if which == 1 else sib
        return remote(block, block, hid_send.at[which, s], hid_recv.at[which, s], to, ten)

    def sum_copy(k, way, t):
        s = lax.rem(k, SEND_SLOTS)
        e = lax.rem(k, RECV_SLOTS)
        return remote(
            outg.at[way, s, t], inc.at[way, e, t], sum_send.at[way, s, t],
            sum_recv.at[way, e, t], above if way == 0 else below, ten,
        )

    def srv_cols(k):
        start = ten * hidden_cols + k * width
        return pl.ds(pl.multiple_of(start, width), width)

    def srv_local(k):
        s = lax.rem(k, 2)
        return pltpu.make_async_copy(served.at[s, ten], serving.at[:, srv_cols(k)], srv_own.at[s])

    def srv_copy(k, d):
        s = lax.rem(k, 2)
        to = lax.rem(ten + d, n_ten)
        return remote(
            served.at[s, to], serving.at[:, srv_cols(k)], srv_send.at[d - 1, s],
            srv_recv.at[d - 1], me, to,
        )

    for d in range(1, GROUP):
        cot_out(d).start()
    for e in range(1, n_ten):
        cot_fwd(0, e).start()
    own_cot().start()
    for copy in acts(0):
        copy.start()
    for copy in opts(0):
        copy.start()

    def step(i, carry):
        @pl.when(i < n)
        def _():
            s = lax.rem(i, HID_SLOTS)
            q = lax.rem(i, 2)
            for copy in acts(i):
                copy.wait()

            @pl.when(i + 1 < n)
            def _():
                for copy in acts(i + 1):
                    copy.start()

            def rows_of(j, c):
                piece = pl.ds(pl.multiple_of(j * 128, 128), 128)
                v = gates[q, piece].astype(jnp.float32)
                u = ups[q, piece].astype(jnp.float32)
                value = (0.5 * v) * (1.0 + jnp.tanh(0.5 * v)) * u
                place = pl.ds(pl.multiple_of(g * tokens + j * 128, 128), 128)
                hid[s, place] = value.astype(jnp.bfloat16)
                return c

            lax.fori_loop(0, tokens // 128, rows_of, 0)

            @pl.when(i >= HID_SLOTS)
            def _():
                pl.semaphore_wait(hid_free.at[0], 1)
                pl.semaphore_wait(hid_free.at[1], 1)

            hid_copy(i, 1).start()
            hid_copy(i, 0).start()

        @pl.when(i == 0)
        def _():
            for d in range(1, GROUP):
                cot_out(d).wait_recv()
                for e in range(1, n_ten):
                    cot_fwd(d, e).start()

        b = i - 1

        @pl.when((b >= 0) & (b < n))
        def _():
            hid_copy(b, 1).wait_recv()
            hid_copy(b, 2).start()

        c = i - 2

        @pl.when(c == 0)
        def _():
            own_cot().wait()
            for d in range(1, GROUP):
                cot_out(d).wait_send()

        @pl.when(c == LATE)
        def _():
            for d in range(GROUP):
                for e in range(1, n_ten):
                    cot_fwd(d, e).wait()

        @pl.when((c >= 0) & (c < n))
        def _():
            s = lax.rem(c, HID_SLOTS)
            hid_copy(c, 0).wait_recv()
            hid_copy(c, 2).wait_recv()

            for which in range(3):
                hid_copy(c, which).wait_send()

        def product(j, carry):
            k = c - jnp.where(j == ten, 0, LATE)

            @pl.when((k >= 0) & (k < n))
            def _():
                half = per * rows
                place = pl.ds(pl.multiple_of(j * half, half), half)
                part[lax.rem(k, part_slots), place] = jnp.dot(
                    cot_all[place], hid[lax.rem(k, HID_SLOTS)], preferred_element_type=jnp.float32
                )

            return carry

        lax.fori_loop(0, n_ten, product, 0)

        @pl.when((c >= LATE) & (c - LATE + HID_SLOTS < n))
        def _():
            pl.semaphore_signal(
                hid_free.at[0], inc=1, device_id=(sib, ten), device_id_type=MESH
            )
            pl.semaphore_signal(
                hid_free.at[1], inc=1, device_id=(far, ten), device_id_type=MESH
            )

        for way in (0, 1):
            hops = rank if way == 0 else last - rank
            source = below if way == 0 else above

            def one_target(t, carry, way=way, hops=hops, source=source):
                k = i - 2 - HOP * hops - lag(t)
                ahead = (t > rank) if way == 0 else (t < rank)

                @pl.when((k >= 0) & (k < n) & (ahead | ((t == rank) & (hops > 0))))
                def _():
                    ps = lax.rem(k, part_slots)
                    es = lax.rem(k, RECV_SLOTS)
                    qs = lax.rem(k, SEND_SLOTS)

                    @pl.when(hops > 0)
                    def _():
                        sum_copy(k, way, t).wait_recv()

                    @pl.when(ahead)
                    def _():
                        @pl.when(k >= SEND_SLOTS)
                        def _():
                            sum_copy(k, way, t).wait_send()

                        @pl.when(hops > 0)
                        def _():
                            def rows_of(j, c):
                                piece = pl.ds(pl.multiple_of(j * big, big), big)
                                value = part[ps, here(t, j, big)] + inc[way, es, t, piece].astype(
                                    jnp.float32
                                )
                                outg[way, qs, t, piece] = value.astype(jnp.bfloat16)
                                return c

                            lax.fori_loop(0, rows // big, rows_of, 0)

                        @pl.when(hops == 0)
                        def _():
                            def rows_of(j, c):
                                piece = pl.ds(pl.multiple_of(j * big, big), big)
                                outg[way, qs, t, piece] = part[ps, here(t, j, big)].astype(jnp.bfloat16)
                                return c

                            lax.fori_loop(0, rows // big, rows_of, 0)

                        @pl.when(k >= RECV_SLOTS)
                        def _():
                            pl.semaphore_wait(sum_free.at[way, t], 1)

                        sum_copy(k, way, t).start()

                    @pl.when(t == rank)
                    def _():
                        def rows_of(j, c):
                            piece = pl.ds(pl.multiple_of(j * big, big), big)
                            part[ps, here(t, j, big)] += inc[way, es, t, piece].astype(jnp.float32)
                            return c

                        lax.fori_loop(0, rows // big, rows_of, 0)

                    @pl.when((hops > 0) & (k + RECV_SLOTS < n))
                    def _():
                        pl.semaphore_signal(
                            sum_free.at[way, t], inc=1, device_id=(source, ten),
                            device_id_type=MESH,
                        )

                return carry

            lax.fori_loop(0, ranks, one_target, 0)

        f = i - 2 - HOP * last - EXTRA - lag(rank)

        @pl.when((f >= 0) & (f < n))
        def _():
            ps = lax.rem(f, part_slots)
            s = lax.rem(f, 2)
            for copy in opts(f):
                copy.wait()

            @pl.when(f + 1 < n)
            def _():
                for copy in opts(f + 1):
                    copy.start()

            @pl.when(f >= 2)
            def _():
                for copy in results(f):
                    copy.wait()
                srv_local(f).wait()
                for d in range(1, n_ten):
                    srv_copy(f, d).wait_send()

            def rows_of(j, c):
                piece = pl.ds(pl.multiple_of(j * small, small), small)
                grad = part[ps, here(rank, j, small)]
                m = 0.9 * opt_in[s, 1, piece] + 0.1 * grad
                v = 0.95 * opt_in[s, 2, piece] + 0.05 * grad * grad
                old = opt_in[s, 0, piece]
                new = old - 0.01 * ((m * FIRST) / (jnp.sqrt(v * SECOND) + 1e-08) + 0.1 * old)
                opt_out[s, 0, piece] = new
                opt_out[s, 1, piece] = m
                opt_out[s, 2, piece] = v
                return c

            lax.fori_loop(0, rows // small, rows_of, 0)
            block = rows // n_ten
            for t in range(n_ten):
                served[s, t] = opt_out[s, 0, t * block : (t + 1) * block].astype(jnp.bfloat16)
            for d in range(1, n_ten):
                srv_copy(f, d).start()
            srv_local(f).start()
            for copy in results(f):
                copy.start()

        return carry

    lax.fori_loop(0, n + 2 + HOP * last + EXTRA + LATE, step, 0)

    for k in range(max(n - 2, 0), n):
        for copy in results(k):
            copy.wait()
        srv_local(k).wait()
        for d in range(1, n_ten):
            srv_copy(k, d).wait_send()
    for k in range(max(n - SEND_SLOTS, 0), n):
        for way in (0, 1):
            def drain(t, carry, way=way, k=k):
                @pl.when((t > rank) if way == 0 else (t < rank))
                def _():
                    sum_copy(k, way, t).wait_send()

                return carry

            lax.fori_loop(0, ranks, drain, 0)
    for d in range(1, n_ten):
        origin = lax.rem(ten + n_ten - d, n_ten)
        area = serving.at[
            :, pl.ds(pl.multiple_of(origin * hidden_cols, hidden_cols), hidden_cols)
        ]
        remote(area, area, srv_send.at[d - 1, 0], srv_recv.at[d - 1], me, origin).wait_recv()


def on_device(n_dp, n_ten, gate_pre, up_pre, out_grad, master, moment_one, moment_two):
    tokens, hidden_cols = gate_pre.shape
    rows = master.shape[0]
    width = 256 if hidden_cols % 256 == 0 else 128
    ranks = n_dp // GROUP
    per = ranks // n_ten
    cot = out_grad.T.reshape(per, GROUP, rows, tokens).swapaxes(0, 1)
    cot = cot.reshape(GROUP, per * rows, tokens)
    part_slots = HOP * (ranks - 1) + 1 + EXTRA
    f32, bf16 = jnp.float32, jnp.bfloat16
    DMA, REG = pltpu.SemaphoreType.DMA, pltpu.SemaphoreType.REGULAR
    scratch = [
        pltpu.VMEM((ranks * rows, GROUP * tokens), bf16),
        pltpu.VMEM((2, tokens, width), bf16),
        pltpu.VMEM((2, tokens, width), bf16),
        pltpu.VMEM((HID_SLOTS, GROUP * tokens, width), bf16),
        pltpu.VMEM((part_slots, ranks * rows, width), f32),
        pltpu.VMEM((2, RECV_SLOTS, ranks, rows, width), bf16),
        pltpu.VMEM((2, SEND_SLOTS, ranks, rows, width), bf16),
        pltpu.VMEM((2, 3, rows, width), f32),
        pltpu.VMEM((2, 3, rows, width), f32),
        pltpu.VMEM((2, n_ten, rows // n_ten, width), bf16),
        DMA((GROUP - 1,)),
        DMA((GROUP - 1,)),
        DMA((n_ten - 1, GROUP)),
        DMA((n_ten - 1, GROUP)),
        DMA,
        DMA((2, 2)),
        DMA((3, HID_SLOTS)),
        DMA((3, HID_SLOTS)),
        REG((2,)),
        DMA((2, SEND_SLOTS, ranks)),
        DMA((2, RECV_SLOTS, ranks)),
        REG((2, ranks)),
        DMA((3, 2)),
        DMA((3, 2)),
        DMA((n_ten - 1, 2)),
        DMA((n_ten - 1,)),
        DMA((2,)),
    ]
    whole = jax.ShapeDtypeStruct((rows, hidden_cols), f32)
    return pl.pallas_call(
        functools.partial(kernel, n_dp, n_ten, width),
        out_shape=(
            whole,
            whole,
            whole,
            jax.ShapeDtypeStruct((rows // n_ten, n_ten * hidden_cols), bf16),
        ),
        in_specs=[pl.BlockSpec(memory_space=pl.ANY)] * 6,
        out_specs=[pl.BlockSpec(memory_space=pl.ANY)] * 4,
        scratch_shapes=scratch,
        compiler_params=pltpu.CompilerParams(
            collective_id=0, has_side_effects=True, vmem_limit_bytes=56 * 2**20
        ),
        cost_estimate=pl.CostEstimate(
            flops=2 * rows * ranks * GROUP * tokens * hidden_cols,
            bytes_accessed=24 * rows * hidden_cols + 4 * tokens * hidden_cols,
            transcendentals=tokens * hidden_cols,
        ),
        name="grad_update",
    )(gate_pre, up_pre, cot, master, moment_one, moment_two)


def solution(mesh):
    placed = (P("dp", "tensor"),) * 6
    return jax.shard_map(
        functools.partial(on_device, mesh.shape["dp"], mesh.shape["tensor"]),
        mesh=mesh,
        in_specs=placed,
        out_specs=(
            P("dp", "tensor"),
            P("dp", "tensor"),
            P("dp", "tensor"),
            P(("dp", "tensor"), None),
        ),
        check_vma=False,
    )
```

```python
import functools

import jax
import jax.numpy as jnp
from jax import lax
from jax.experimental import pallas as pl
from jax.experimental.pallas import tpu as pltpu
from jax.sharding import PartitionSpec as P

MESH = pl.DeviceIdType.MESH
GROUP = 4
LATE = 4
HID_SLOTS = 4 + LATE
RECV_SLOTS = 5
SEND_SLOTS = 3
HOP = 2
EXTRA = 0
FIRST = 1.0 / (1.0 - 0.9**20)
SECOND = 1.0 / (1.0 - 0.95**20)


def kernel(
    n_dp,
    n_ten,
    width,
    gate,
    up,
    cot,
    master,
    one,
    two,
    master_out,
    one_out,
    two_out,
    serving,
    cot_all,
    gates,
    ups,
    hid,
    part,
    inc,
    outg,
    opt_in,
    opt_out,
    served,
    cot_send,
    cot_recv,
    fwd_send,
    fwd_recv,
    own_sem,
    act_sem,
    hid_send,
    hid_recv,
    hid_free,
    sum_send,
    sum_recv,
    sum_free,
    opt_sem,
    res_sem,
    srv_send,
    srv_recv,
    srv_own,
):
    tokens, hidden_cols = gate.shape
    rows = master.shape[0]
    n = hidden_cols // width
    ranks = n_dp // GROUP
    per = ranks // n_ten
    part_slots = part.shape[0]
    last = ranks - 1

    me = lax.axis_index("dp")
    ten = lax.axis_index("tensor")
    rank = lax.div(me, GROUP)
    g = lax.rem(me, GROUP)
    sib = me + 1 - 2 * lax.rem(g, 2)
    far = me + 2 - 4 * lax.div(g, 2)
    g_far = g + 2 - 4 * lax.div(g, 2)
    g_sib = g + 1 - 2 * lax.rem(g, 2)
    near = [g, g_sib, g_far, g_far + g_sib - g]
    peers = [rank * GROUP + who for who in near[1:]]
    partners = [lax.rem(ten + d, n_ten) for d in range(1, n_ten)]
    below = me - GROUP
    above = me + GROUP

    barrier = pltpu.get_barrier_semaphore()
    for peer in peers:
        pl.semaphore_signal(barrier, inc=1, device_id=(peer, ten), device_id_type=MESH)
    for partner in partners:
        pl.semaphore_signal(barrier, inc=1, device_id=(me, partner), device_id_type=MESH)
    for step in (1, ranks - 1):
        other = lax.rem(rank + step, ranks) * GROUP + g
        pl.semaphore_signal(barrier, inc=1, device_id=(other, ten), device_id_type=MESH)
    pl.semaphore_wait(barrier, len(peers) + len(partners) + 2)

    def lag(t):
        return jnp.where(lax.div(t, per) == ten, 0, LATE)

    big, small = rows // 2, rows // 5

    def here(t, j, size):
        return pl.ds(pl.multiple_of(t * rows + j * size, 16), size)

    def cols(k):
        return pl.ds(pl.multiple_of(k * width, width), width)

    def toks(who):
        return pl.ds(pl.multiple_of(who * tokens, tokens), tokens)

    def remote(src, dst, send, recv, dp, tensor):
        return pltpu.make_async_remote_copy(
            src_ref=src,
            dst_ref=dst,
            send_sem=send,
            recv_sem=recv,
            device_id=(dp, tensor),
            device_id_type=MESH,
        )

    def cot_here(who):
        half = per * rows
        return cot_all.at[pl.ds(pl.multiple_of(ten * half, half), half), toks(who)]

    def cot_out(d):
        to = near[d]
        return remote(
            cot.at[to], cot_here(g), cot_send.at[d - 1], cot_recv.at[d - 1],
            rank * GROUP + to, ten,
        )

    def cot_fwd(d, e):
        src = cot.at[g] if d == 0 else cot_here(near[d])
        return remote(
            src, cot_here(near[d]),
            fwd_send.at[e - 1, d], fwd_recv.at[e - 1, d], me, lax.rem(ten + e, n_ten),
        )

    def own_cot():
        return pltpu.make_async_copy(cot.at[g], cot_here(g), own_sem)

    def acts(k):
        s = lax.rem(k, 2)
        return (
            pltpu.make_async_copy(gate.at[:, cols(k)], gates.at[s], act_sem.at[0, s]),
            pltpu.make_async_copy(up.at[:, cols(k)], ups.at[s], act_sem.at[1, s]),
        )

    def opts(k):
        s = lax.rem(k, 2)
        return [
            pltpu.make_async_copy(ref.at[:, cols(k)], opt_in.at[s, j], opt_sem.at[j, s])
            for j, ref in enumerate((master, one, two))
        ]

    def results(k):
        s = lax.rem(k, 2)
        return [
            pltpu.make_async_copy(opt_out.at[s, j], ref.at[:, cols(k)], res_sem.at[j, s])
            for j, ref in enumerate((master_out, one_out, two_out))
        ]

    def hid_copy(k, which):
        s = lax.rem(k, HID_SLOTS)
        block = hid.at[s, toks(g_far if which == 2 else g)]
        to = far if which == 1 else sib
        return remote(block, block, hid_send.at[which, s], hid_recv.at[which, s], to, ten)

    def sum_copy(k, way, t):
        s = lax.rem(k, SEND_SLOTS)
        e = lax.rem(k, RECV_SLOTS)
        return remote(
            outg.at[way, s, t], inc.at[way, e, t], sum_send.at[way, s, t],
            sum_recv.at[way, e, t], above if way == 0 else below, ten,
        )

    def srv_cols(k):
        start = ten * hidden_cols + k * width
        return pl.ds(pl.multiple_of(start, width), width)

    def srv_local(k):
        s = lax.rem(k, 2)
        return pltpu.make_async_copy(served.at[s, ten], serving.at[:, srv_cols(k)], srv_own.at[s])

    def srv_copy(k, d):
        s = lax.rem(k, 2)
        to = lax.rem(ten + d, n_ten)
        return remote(
            served.at[s, to], serving.at[:, srv_cols(k)], srv_send.at[d - 1, s],
            srv_recv.at[d - 1], me, to,
        )

    for d in range(1, GROUP):
        cot_out(d).start()
    for e in range(1, n_ten):
        cot_fwd(0, e).start()
    own_cot().start()
    for copy in acts(0):
        copy.start()
    for copy in opts(0):
        copy.start()

    def step(i, carry):
        @pl.when(i < n)
        def _():
            s = lax.rem(i, HID_SLOTS)
            q = lax.rem(i, 2)
            for copy in acts(i):
                copy.wait()

            @pl.when(i + 1 < n)
            def _():
                for copy in acts(i + 1):
                    copy.start()

            def rows_of(j, c):
                piece = pl.ds(pl.multiple_of(j * 128, 128), 128)
                v = gates[q, piece].astype(jnp.float32)
                u = ups[q, piece].astype(jnp.float32)
                value = (0.5 * v) * (1.0 + jnp.tanh(0.5 * v)) * u
                place = pl.ds(pl.multiple_of(g * tokens + j * 128, 128), 128)
                hid[s, place] = value.astype(jnp.bfloat16)
                return c

            lax.fori_loop(0, tokens // 128, rows_of, 0)

            @pl.when(i >= HID_SLOTS)
            def _():
                pl.semaphore_wait(hid_free.at[0], 1)
                pl.semaphore_wait(hid_free.at[1], 1)

            hid_copy(i, 1).start()
            hid_copy(i, 0).start()

        @pl.when(i == 0)
        def _():
            for d in range(1, GROUP):
                cot_out(d).wait_recv()
                for e in range(1, n_ten):
                    cot_fwd(d, e).start()

        b = i - 1

        @pl.when((b >= 0) & (b < n))
        def _():
            hid_copy(b, 1).wait_recv()
            hid_copy(b, 2).start()

        c = i - 2

        @pl.when(c == 0)
        def _():
            own_cot().wait()
            for d in range(1, GROUP):
                cot_out(d).wait_send()

        @pl.when(c == LATE)
        def _():
            for d in range(GROUP):
                for e in range(1, n_ten):
                    cot_fwd(d, e).wait()

        @pl.when((c >= 0) & (c < n))
        def _():
            s = lax.rem(c, HID_SLOTS)
            hid_copy(c, 0).wait_recv()
            hid_copy(c, 2).wait_recv()

            for which in range(3):
                hid_copy(c, which).wait_send()

        def product(j, carry):
            k = c - jnp.where(j == ten, 0, LATE)

            @pl.when((k >= 0) & (k < n))
            def _():
                half = per * rows
                place = pl.ds(pl.multiple_of(j * half, half), half)
                part[lax.rem(k, part_slots), place] = jnp.dot(
                    cot_all[place], hid[lax.rem(k, HID_SLOTS)], preferred_element_type=jnp.float32
                )

            return carry

        lax.fori_loop(0, n_ten, product, 0)

        @pl.when((c >= LATE) & (c - LATE + HID_SLOTS < n))
        def _():
            pl.semaphore_signal(
                hid_free.at[0], inc=1, device_id=(sib, ten), device_id_type=MESH
            )
            pl.semaphore_signal(
                hid_free.at[1], inc=1, device_id=(far, ten), device_id_type=MESH
            )

        for way in (0, 1):
            hops = rank if way == 0 else last - rank
            source = below if way == 0 else above

            def one_target(j, carry, way=way, hops=hops, source=source):
                t = last - j if way == 0 else j
                k = i - 2 - HOP * hops - lag(t)
                ahead = (t > rank) if way == 0 else (t < rank)

                @pl.when((k >= 0) & (k < n) & (ahead | ((t == rank) & (hops > 0))))
                def _():
                    ps = lax.rem(k, part_slots)
                    es = lax.rem(k, RECV_SLOTS)
                    qs = lax.rem(k, SEND_SLOTS)

                    @pl.when(hops > 0)
                    def _():
                        sum_copy(k, way, t).wait_recv()

                    @pl.when(ahead)
                    def _():
                        @pl.when(k >= SEND_SLOTS)
                        def _():
                            sum_copy(k, way, t).wait_send()

                        @pl.when(hops > 0)
                        def _():
                            def rows_of(h, c):
                                piece = pl.ds(pl.multiple_of(h * big, big), big)
                                value = part[ps, here(t, h, big)] + inc[way, es, t, piece].astype(
                                    jnp.float32
                                )
                                outg[way, qs, t, piece] = value.astype(jnp.bfloat16)
                                return c

                            lax.fori_loop(0, rows // big, rows_of, 0)

                        @pl.when(hops == 0)
                        def _():
                            def rows_of(h, c):
                                piece = pl.ds(pl.multiple_of(h * big, big), big)
                                outg[way, qs, t, piece] = part[ps, here(t, h, big)].astype(jnp.bfloat16)
                                return c

                            lax.fori_loop(0, rows // big, rows_of, 0)

                        @pl.when(k >= RECV_SLOTS)
                        def _():
                            pl.semaphore_wait(sum_free.at[way, t], 1)

                        sum_copy(k, way, t).start()

                    @pl.when(t == rank)
                    def _():
                        def rows_of(h, c):
                            piece = pl.ds(pl.multiple_of(h * big, big), big)
                            part[ps, here(t, h, big)] += inc[way, es, t, piece].astype(jnp.float32)
                            return c

                        lax.fori_loop(0, rows // big, rows_of, 0)

                    @pl.when((hops > 0) & (k + RECV_SLOTS < n))
                    def _():
                        pl.semaphore_signal(
                            sum_free.at[way, t], inc=1, device_id=(source, ten),
                            device_id_type=MESH,
                        )

                return carry

            lax.fori_loop(0, ranks, one_target, 0)

        f = i - 2 - HOP * last - EXTRA - lag(rank)

        @pl.when((f >= 0) & (f < n))
        def _():
            ps = lax.rem(f, part_slots)
            s = lax.rem(f, 2)
            for copy in opts(f):
                copy.wait()

            @pl.when(f + 1 < n)
            def _():
                for copy in opts(f + 1):
                    copy.start()

            @pl.when(f >= 2)
            def _():
                for copy in results(f):
                    copy.wait()
                srv_local(f).wait()
                for d in range(1, n_ten):
                    srv_copy(f, d).wait_send()

            def rows_of(j, c):
                piece = pl.ds(pl.multiple_of(j * small, small), small)
                grad = part[ps, here(rank, j, small)]
                m = 0.9 * opt_in[s, 1, piece] + 0.1 * grad
                v = 0.95 * opt_in[s, 2, piece] + 0.05 * grad * grad
                old = opt_in[s, 0, piece]
                new = old - 0.01 * ((m * FIRST) / (jnp.sqrt(v * SECOND) + 1e-08) + 0.1 * old)
                opt_out[s, 0, piece] = new
                opt_out[s, 1, piece] = m
                opt_out[s, 2, piece] = v
                return c

            lax.fori_loop(0, rows // small, rows_of, 0)
            block = rows // n_ten
            for t in range(n_ten):
                served[s, t] = opt_out[s, 0, t * block : (t + 1) * block].astype(jnp.bfloat16)
            for d in range(1, n_ten):
                srv_copy(f, d).start()
            srv_local(f).start()
            for copy in results(f):
                copy.start()

        return carry

    lax.fori_loop(0, n + 2 + HOP * last + EXTRA + LATE, step, 0)

    for k in range(max(n - 2, 0), n):
        for copy in results(k):
            copy.wait()
        srv_local(k).wait()
        for d in range(1, n_ten):
            srv_copy(k, d).wait_send()
    for k in range(max(n - SEND_SLOTS, 0), n):
        for way in (0, 1):
            def drain(t, carry, way=way, k=k):
                @pl.when((t > rank) if way == 0 else (t < rank))
                def _():
                    sum_copy(k, way, t).wait_send()

                return carry

            lax.fori_loop(0, ranks, drain, 0)
    for d in range(1, n_ten):
        origin = lax.rem(ten + n_ten - d, n_ten)
        area = serving.at[
            :, pl.ds(pl.multiple_of(origin * hidden_cols, hidden_cols), hidden_cols)
        ]
        remote(area, area, srv_send.at[d - 1, 0], srv_recv.at[d - 1], me, origin).wait_recv()


def on_device(n_dp, n_ten, gate_pre, up_pre, out_grad, master, moment_one, moment_two):
    tokens, hidden_cols = gate_pre.shape
    rows = master.shape[0]
    width = 256 if hidden_cols % 256 == 0 else 128
    ranks = n_dp // GROUP
    per = ranks // n_ten
    cot = out_grad.T.reshape(per, GROUP, rows, tokens).swapaxes(0, 1)
    cot = cot.reshape(GROUP, per * rows, tokens)
    part_slots = HOP * (ranks - 1) + 1 + EXTRA
    f32, bf16 = jnp.float32, jnp.bfloat16
    DMA, REG = pltpu.SemaphoreType.DMA, pltpu.SemaphoreType.REGULAR
    scratch = [
        pltpu.VMEM((ranks * rows, GROUP * tokens), bf16),
        pltpu.VMEM((2, tokens, width), bf16),
        pltpu.VMEM((2, tokens, width), bf16),
        pltpu.VMEM((HID_SLOTS, GROUP * tokens, width), bf16),
        pltpu.VMEM((part_slots, ranks * rows, width), f32),
        pltpu.VMEM((2, RECV_SLOTS, ranks, rows, width), bf16),
        pltpu.VMEM((2, SEND_SLOTS, ranks, rows, width), bf16),
        pltpu.VMEM((2, 3, rows, width), f32),
        pltpu.VMEM((2, 3, rows, width), f32),
        pltpu.VMEM((2, n_ten, rows // n_ten, width), bf16),
        DMA((GROUP - 1,)),
        DMA((GROUP - 1,)),
        DMA((n_ten - 1, GROUP)),
        DMA((n_ten - 1, GROUP)),
        DMA,
        DMA((2, 2)),
        DMA((3, HID_SLOTS)),
        DMA((3, HID_SLOTS)),
        REG((2,)),
        DMA((2, SEND_SLOTS, ranks)),
        DMA((2, RECV_SLOTS, ranks)),
        REG((2, ranks)),
        DMA((3, 2)),
        DMA((3, 2)),
        DMA((n_ten - 1, 2)),
        DMA((n_ten - 1,)),
        DMA((2,)),
    ]
    whole = jax.ShapeDtypeStruct((rows, hidden_cols), f32)
    return pl.pallas_call(
        functools.partial(kernel, n_dp, n_ten, width),
        out_shape=(
            whole,
            whole,
            whole,
            jax.ShapeDtypeStruct((rows // n_ten, n_ten * hidden_cols), bf16),
        ),
        in_specs=[pl.BlockSpec(memory_space=pl.ANY)] * 6,
        out_specs=[pl.BlockSpec(memory_space=pl.ANY)] * 4,
        scratch_shapes=scratch,
        compiler_params=pltpu.CompilerParams(
            collective_id=0, has_side_effects=True, vmem_limit_bytes=56 * 2**20
        ),
        cost_estimate=pl.CostEstimate(
            flops=2 * rows * ranks * GROUP * tokens * hidden_cols,
            bytes_accessed=24 * rows * hidden_cols + 4 * tokens * hidden_cols,
            transcendentals=tokens * hidden_cols,
        ),
        name="grad_update",
    )(gate_pre, up_pre, cot, master, moment_one, moment_two)


def solution(mesh):
    placed = (P("dp", "tensor"),) * 6
    return jax.shard_map(
        functools.partial(on_device, mesh.shape["dp"], mesh.shape["tensor"]),
        mesh=mesh,
        in_specs=placed,
        out_specs=(
            P("dp", "tensor"),
            P("dp", "tensor"),
            P("dp", "tensor"),
            P(("dp", "tensor"), None),
        ),
        check_vma=False,
    )
```
